32 devices in a mesh: sec: 16 (over z, y, x), mpo: 2 (over core).
Axes of the slice: x: 2, y: 2, z: 4, core: 2. Of those that a mesh axis runs over, the one named last changes fastest.
Arguments:
- wavefunction: bfloat16 [16, 8, 512, 256], P('sec', None, 'mpo'), may hold values from -6 to 6
- left_env: bfloat16 [16, 40, 512, 512], P('sec', 'mpo'), may hold values from -0.0390625 to 0.0390625
- right_env: bfloat16 [16, 40, 256, 256], P('sec', 'mpo'), may hold values from -0.375 to 0.375
- left_dims: int32 [16], P('sec'), may hold values from 256 to 512
- right_dims: int32 [16], P('sec'), may hold values from 128 to 256
- term_shift: int32 [40], P('mpo'), may hold values from 0 to 4, as said below
Outputs:
- product: bfloat16 [16, 8, 512, 256], P('sec', None, 'mpo')
The draws below stay inside these ranges and needn't reach their ends.
Inputs may be any that keep to these rules, and one draw needn't show every extreme that they name: `term_shift`: each of the five classes is named by exactly 8 terms.
All inputs are finite; a program needn't handle non-finite values.
Results may differ from the reference program's by a relative error of at most 0.0049.
Values may be sent and summed in bfloat16 or wider, within the bound.
No kernel may reach another device: no remote copies, remote signals or barrier semaphores. Data moves between devices by JAX's collectives and lax.ppermute only.
A program may use at most 192 MiB of HBM per device.

```python
import jax
import jax.numpy as jnp
from jax import lax

P_SIZE = 512
Q = 256
TERMS = 40
SPINS = 8
NVEC = 8
SECTORS = 16


def draw_left_dims(key, part):
    drawn = jax.random.randint(key, (SECTORS,), P_SIZE // 2, P_SIZE + 1).astype(jnp.int32)
    return drawn.at[0].set(P_SIZE).at[1].set(P_SIZE // 2)


def draw_right_dims(key, part):
    drawn = jax.random.randint(key, (SECTORS,), Q // 2, Q + 1).astype(jnp.int32)
    return drawn.at[1].set(Q).at[0].set(Q // 2)


def draw_term_shift(key, part):
    return (jax.random.permutation(key, TERMS) % 5).astype(jnp.int32)


def steps_of(rng, extent, pieces, least, largest):
    gain, own = 1.0, jax.random.fold_in(rng, 6)
    for position, shards_of in pieces:
        steps = jnp.exp(jax.random.uniform(jax.random.fold_in(own, position), (shards_of,), jnp.float32, least / len(pieces), largest / len(pieces)))
        gain = gain * jnp.repeat(steps, extent[position] // shards_of).reshape([-1 if axis == position else 1 for axis in range(len(extent))])
    return gain


def centred(key, extent, deviation, reach, cuts=(), kind=jnp.bfloat16):
    array = deviation * jax.random.normal(key, extent, jnp.float32)
    if cuts:
        array = array * steps_of(key, extent, cuts, -0.22, 0.18)
    return jnp.clip(array, -reach, reach).astype(kind)


def setup_inputs(seed: int = 0) -> dict:
    keys = jax.random.split(jax.random.key(seed), 7)
    return {
        "wavefunction": centred(keys[0], (SECTORS, NVEC, P_SIZE, Q), 1.0, 6.0, ((0, 16), (2, 2))),
        "left_env": centred(keys[1], (SECTORS, TERMS, P_SIZE, P_SIZE), (P_SIZE * TERMS) ** -0.5, 0.0390625, ((0, 16), (1, 2))),
        "right_env": centred(keys[2], (SECTORS, TERMS, Q, Q), Q ** -0.5, 0.375, ((0, 16), (1, 2))),
        "left_dims": draw_left_dims(jax.random.fold_in(keys[6], 71), 0),
        "right_dims": draw_right_dims(jax.random.fold_in(keys[6], 71), 0),
        "term_shift": draw_term_shift(jax.random.fold_in(keys[6], 71), 0),
    }


number_steps = (0, 1, -1, 1, -1)
spin_steps = (0, 1, -1, -1, 1)


def reference(wavefunction, left_env, right_env, left_dims, right_dims, term_shift):
    row_ids = jnp.arange(P_SIZE, dtype=jnp.int32)
    column_ids = jnp.arange(Q, dtype=jnp.int32)
    row_mask = row_ids[None, :] < left_dims[:, None]
    column_mask = column_ids[None, :] < right_dims[:, None]
    keep_mask = row_mask[:, None, :, None] & column_mask[:, None, None, :]
    live_block = jnp.where(keep_mask, wavefunction, jnp.zeros_like(wavefunction))
    selector = (term_shift[:, None] == jnp.arange(5, dtype=jnp.int32)[None, :]).astype(jnp.float32)
    lattice_rows = SECTORS // SPINS

    def one_sector(sector_id):
        sector_line = sector_id // SPINS
        sector_place = sector_id % SPINS
        sources = []
        for shift_class in range(5):
            source_line = sector_line - number_steps[shift_class]
            source_place = sector_place - spin_steps[shift_class]
            inside = (source_line >= 0) & (source_line < lattice_rows) & (source_place >= 0) & (source_place < SPINS)
            source_id = jnp.clip(source_line * SPINS + source_place, 0, SECTORS - 1).astype(jnp.int32)
            neighbour = lax.dynamic_index_in_dim(live_block, source_id, 0, keepdims=False).astype(jnp.float32)
            sources.append(neighbour * inside.astype(jnp.float32))
        stacked = jnp.stack(sources)
        selected = jnp.einsum('tc,cvpq->tvpq', selector, stacked)
        left_block = lax.dynamic_index_in_dim(left_env, sector_id, 0, keepdims=False).astype(jnp.float32)
        right_block = lax.dynamic_index_in_dim(right_env, sector_id, 0, keepdims=False).astype(jnp.float32)
        applied = jnp.einsum('tpk,tvkq->tvpq', left_block, selected).astype(jnp.bfloat16)
        applied = lax.optimization_barrier(applied).astype(jnp.float32)
        return jnp.einsum('tvpk,tqk->vpq', applied, right_block)

    total = lax.map(one_sector, jnp.arange(SECTORS, dtype=jnp.int32))
    return jnp.where(keep_mask, total, jnp.zeros_like(total)).astype(jnp.bfloat16)
```

```python
import functools

import jax
import jax.numpy as jnp
from jax import lax
from jax.experimental import pallas as pl
from jax.experimental.pallas import tpu as pltpu
from jax.sharding import PartitionSpec as P

SPINS = 8
CLASSES = 5


def sum_terms(slots, ways, resume, finish, mask, group, shift_ref, meta_ref, *refs):
    parts, refs = refs[:ways], refs[ways:]
    left_ref, right_ref, refs = refs[0], refs[1], refs[2:]
    if resume is not None:
        before_ref, refs = refs[0], refs[1:]
    if finish:
        keep_ref, give_refs, refs = refs[0], refs[1:ways], refs[ways:]
    else:
        total, refs = refs[0], refs[1:]
    left_buf, right_buf, source, applied, refs = refs[0], refs[1], refs[2], refs[3], refs[4:]
    if finish:
        total, refs = refs[0], refs[1:]
    left_sem, right_sem, part_sem, before_sem = refs
    place, shift_class = meta_ref[0], meta_ref[1]
    vectors, share, columns = parts[0].shape
    rows = share * ways

    def copy_part(turn):
        begin = pl.multiple_of(lax.rem(place + ways - turn, ways) * share, share)
        return pltpu.make_async_copy(parts[turn], source.at[:, pl.ds(begin, share), :], part_sem.at[turn])

    def copies(term, slot):
        return (
            pltpu.make_async_copy(left_ref.at[0, term], left_buf.at[slot], left_sem.at[slot]),
            pltpu.make_async_copy(right_ref.at[0, term], right_buf.at[slot], right_sem.at[slot]),
        )

    for turn in range(ways):
        copy_part(turn).start()

    def fetch(term, count):
        hit = (shift_ref[term] == shift_class) & (count < slots)

        @pl.when(hit)
        def _():
            for copy in copies(term, count):
                copy.start()

        return count + hit.astype(jnp.int32)

    count = lax.fori_loop(0, shift_ref.shape[0], fetch, jnp.int32(0))
    if resume is not None:
        copy_before = pltpu.make_async_copy(before_ref.at[pl.ds(resume, vectors)], total, before_sem)
        copy_before.start()
        copy_before.wait()
    else:
        total[...] = jnp.zeros_like(total)
    for turn in range(ways):
        copy_part(turn).wait()

    if mask:
        kept = (lax.broadcasted_iota(jnp.int32, source.shape[1:], 0) < meta_ref[2]) & (lax.broadcasted_iota(jnp.int32, source.shape[1:], 1) < meta_ref[3])
        for vector in range(vectors):
            source[vector] = jnp.where(kept, source[vector], jnp.zeros_like(source[vector]))

    def arrive(slot):
        for copy in copies(0, slot):
            copy.wait()

    def add_terms(first, group):
        rights = jnp.concatenate([right_buf[first + i] for i in range(group)], axis=1)
        for vector in range(vectors):
            for i in range(group):
                applied[vector, :, i * columns : (i + 1) * columns] = jnp.dot(
                    left_buf[first + i], source[vector], preferred_element_type=jnp.float32
                ).astype(jnp.bfloat16)
        width = group * columns
        total[...] += lax.dot_general(
            applied[:, :, :width].reshape(vectors * rows, width),
            rights,
            (((1,), (1,)), ((), ())),
            preferred_element_type=jnp.float32,
        ).reshape(total.shape)

    whole = count // group

    @pl.loop(0, whole)
    def _(turn):
        for i in range(group):
            arrive(turn * group + i)
        add_terms(turn * group, group)

    if group > 1:

        @pl.loop(whole * group, count)
        def _(slot):
            arrive(slot)
            add_terms(slot, 1)

    if finish:
        for turn in range(ways):
            begin = pl.multiple_of(lax.rem(place + turn, ways) * share, share)
            block = total[:, pl.ds(begin, share), :]
            if turn == 0:
                keep_ref[...] = block
            else:
                give_refs[turn - 1][...] = block.astype(jnp.bfloat16)


def call_terms(shift, meta, parts, left, right, before=None, start=0, finish=False, mask=False):
    ways = len(parts)
    vectors, share, columns = parts[0].shape
    rows = share * ways
    terms = left.shape[1]
    slots = min(terms, terms * ways // CLASSES)
    group = 1 if vectors >= 4 else 2
    any_spec = pl.BlockSpec(memory_space=pl.ANY)
    smem = pl.BlockSpec(memory_space=pltpu.SMEM)
    vmem = pl.BlockSpec(memory_space=pltpu.VMEM)
    operands = [shift, meta, *parts, left, right]
    in_specs = [smem, smem] + [any_spec] * (ways + 2)
    if before is not None:
        operands.append(before)
        in_specs.append(any_spec)
    whole = jax.ShapeDtypeStruct((vectors, rows, columns), jnp.float32)
    scratch = [
        pltpu.VMEM((slots, rows, rows), jnp.bfloat16),
        pltpu.VMEM((slots, columns, columns), jnp.bfloat16),
        pltpu.VMEM((vectors, rows, columns), jnp.bfloat16),
        pltpu.VMEM((vectors, rows, group * columns), jnp.bfloat16),
    ]
    if finish:
        out_shape = [jax.ShapeDtypeStruct((vectors, share, columns), jnp.float32)] + [
            jax.ShapeDtypeStruct((vectors, share, columns), jnp.bfloat16)
        ] * (ways - 1)
        out_specs = [vmem] * ways
        scratch.append(pltpu.VMEM(whole.shape, whole.dtype))
    else:
        out_shape, out_specs = whole, vmem
    scratch += [
        pltpu.SemaphoreType.DMA((slots,)),
        pltpu.SemaphoreType.DMA((slots,)),
        pltpu.SemaphoreType.DMA((ways,)),
        pltpu.SemaphoreType.DMA,
    ]
    typical = max(1, slots // ways)
    return pl.pallas_call(
        functools.partial(sum_terms, slots, ways, None if before is None else start, finish, mask, group),
        out_shape=out_shape,
        in_specs=in_specs,
        out_specs=out_specs,
        scratch_shapes=scratch,
        compiler_params=pltpu.CompilerParams(vmem_limit_bytes=40 * 2**20),
        cost_estimate=pl.CostEstimate(
            flops=typical * vectors * 2 * rows * columns * (rows + columns),
            bytes_accessed=typical * 2 * (rows * rows + columns * columns),
            transcendentals=0,
        ),
    )(*operands)


def permute(array, axis, pairs):
    return lax.ppermute(array, axis, sorted(pairs)) if pairs else jnp.zeros_like(array)


def around(array):
    ways = lax.axis_size("mpo")
    return [array] + [
        permute(array, "mpo", [(i, (i + turn) % ways) for i in range(ways)]) for turn in range(1, ways)
    ]


def per_device(wavefunction, left_env, right_env, left_dims, right_dims, term_shift):
    vectors, share, columns = wavefunction.shape[1:]
    place = lax.axis_index("mpo")
    ways = lax.axis_size("mpo")
    sector = lax.axis_index("sec")
    lines = lax.axis_size("sec") // SPINS
    line, spin = sector // SPINS, sector % SPINS
    odd = spin % 2 == 1
    row_ids = place * share + jnp.arange(share, dtype=jnp.int32)
    column_ids = jnp.arange(columns, dtype=jnp.int32)
    keep_mask = ((row_ids[:, None] < left_dims[0]) & (column_ids[None, :] < right_dims[0]))[None]

    def cross(step):
        return [
            (n * SPINS + p, (n + step) * SPINS + (p ^ 1))
            for n in range(lines)
            for p in range(SPINS)
            if 0 <= n + step < lines
        ]

    relay = [
        (n * SPINS + p, n * SPINS + p + (-2 if p % 2 else 2))
        for n in range(lines)
        for p in range(SPINS)
        if 0 <= p + (-2 if p % 2 else 2) < SPINS
    ]
    relay_here = jnp.where(odd, spin + 2 < SPINS, spin >= 2)
    from_below = (jnp.where(odd, 1, 3), jnp.where(odd, 3, 1), line > 0)
    from_above = (jnp.where(odd, 4, 2), jnp.where(odd, 2, 4), line + 1 < lines)
    if lines == 2:
        ways_across = [(cross(1) + cross(-1), tuple(jnp.where(line == 1, b, a) for b, a in zip(from_below, from_above)))]
    else:
        ways_across = [(cross(1), from_below), (cross(-1), from_above)] if lines > 1 else []

    def meta(shift_class, valid=True):
        return jnp.stack([place, jnp.where(valid, shift_class, -1), left_dims[0], right_dims[0]]).astype(jnp.int32)

    def after(array, *others):
        return lax.optimization_barrier((array, *others))[0]

    terms = functools.partial(call_terms, term_shift)
    widths = [vectors // 4] * 4 if vectors % 4 == 0 else [vectors]
    starts = [sum(widths[:i]) for i in range(len(widths))]
    count = len(widths)
    landed, near_parts, far_parts = {}, {}, {}
    last = None

    def send(index, *behind):
        block = wavefunction[0, starts[index] : starts[index] + widths[index]]
        if behind:
            block = after(block, *behind)
        block = jnp.where(keep_mask, block, jnp.zeros_like(block))
        landed[index] = [permute(block, "sec", pairs) for pairs, _ in ways_across]

    for index in range(min(2, count)):
        send(index)
    own = terms(meta(jnp.int32(0)), around(wavefunction[0]), left_env, right_env, mask=True)
    product = jnp.zeros_like(wavefunction[0])
    totals = {}

    def arrive(index, behind):
        here = [after(block, behind) for block in landed[index]]
        if index + 2 < count:
            send(index + 2, *here)
        near_parts[index] = [around(block) for block in here]
        far_parts[index] = [around(permute(block, "sec", relay)) for block in here]

    def near_terms(index):
        total, offset = own, starts[index]
        for parts, (_, (near, _, valid)) in zip(near_parts[index], ways_across):
            total = terms(meta(near, valid), parts, left_env, right_env, total, offset)
            offset = 0
        totals[index] = (total, offset)
        return total

    def far_terms(index, behind):
        total, offset = totals[index]
        for number, (parts, (_, (_, far, valid))) in enumerate(zip(far_parts[index], ways_across)):
            parts = [after(part, behind) for part in parts]
            total = terms(
                meta(far, valid & relay_here), parts, left_env, right_env, total, offset,
                number == len(ways_across) - 1,
            )
            offset = 0
        return total

    def close(index, sums, product):
        total = sums[0]
        for turn, given in enumerate(sums[1:], 1):
            total += permute(given, "mpo", [(i, (i + turn) % ways) for i in range(ways)]).astype(jnp.float32)
        block = jnp.where(keep_mask, total, jnp.zeros_like(total)).astype(jnp.bfloat16)
        return lax.dynamic_update_slice(product, block, (starts[index], 0, 0))

    before = own
    for index in range(count):
        arrive(index, before)
        before = near_terms(index)
        if index:
            sums = far_terms(index - 1, before)
            before = sums[0]
            product = close(index - 1, sums, product)
    product = close(count - 1, far_terms(count - 1, before), product)
    return product[None]


def solution(mesh):
    in_specs = (
        P("sec", None, "mpo", None),
        P("sec", "mpo", None, None),
        P("sec", "mpo", None, None),
        P("sec"),
        P("sec"),
        P("mpo"),
    )
    out_specs = P("sec", None, "mpo", None)
    return jax.shard_map(
        per_device, mesh=mesh, in_specs=in_specs, out_specs=out_specs, check_vma=False
    )
```

```python
import functools

import jax
import jax.numpy as jnp
from jax import lax
from jax.experimental import pallas as pl
from jax.experimental.pallas import tpu as pltpu
from jax.sharding import PartitionSpec as P

SPINS = 8
CLASSES = 5
SPARE = 0
VMEM = 40 * 2**20
WHOLE_VMEM = 62 * 2**20
RUNS = (4, 4)
PLACE, LEFT, RIGHT, LIVE, OWN = 0, 1, 2, 3, 3 + CLASSES
HINT = pl.CostEstimate(flops=10**6, bytes_accessed=10**3, transcendentals=0)


def sharing(shift_ref, meta_ref, terms, ways, spare):
    both = terms * ways // CLASSES
    half = both // 2

    def tally(term, counts):
        return tuple(n + (shift_ref[term] == c).astype(jnp.int32) for c, n in enumerate(counts))

    counts = lax.fori_loop(0, terms, tally, (jnp.int32(0),) * CLASSES)
    given_before, taken_before, plan = jnp.int32(0), jnp.int32(0), []
    for c, count in enumerate(counts):
        live = meta_ref[LIVE + c]
        surplus = jnp.maximum(count - half, 0) * live
        lack = jnp.maximum(both - half - (count if both % 2 == 0 else count), 0) * live
        given = jnp.clip(spare - given_before, 0, surplus)
        taken = jnp.clip(spare - taken_before, 0, lack)
        plan.append((count - given, given_before, given, taken_before, taken))
        given_before, taken_before = given_before + surplus, taken_before + lack
    return plan


def chosen(plan, shift_class, entry):
    value = jnp.int32(0)
    for c, entries in enumerate(plan):
        value = jnp.where(shift_class == c, entries[entry], value)
    return value


def pack_terms(spare, ways, shift_ref, meta_ref, left_ref, right_ref, _, lefts, rights, left_sem, right_sem):
    terms = shift_ref.shape[0]
    plan = sharing(shift_ref, meta_ref, terms, ways, spare)

    def copies(term, slot):
        return (
            pltpu.make_async_copy(left_ref.at[0, term], lefts.at[slot], left_sem.at[slot]),
            pltpu.make_async_copy(right_ref.at[0, term], rights.at[slot], right_sem.at[slot]),
        )

    def step(term, ranks):
        c = shift_ref[term]
        rank = jnp.int32(0)
        for number, seen in enumerate(ranks):
            rank = jnp.where(c == number, seen, rank)
        beyond = rank - chosen(plan, c, 0)
        slot = chosen(plan, c, 1) + beyond

        @pl.when((beyond >= 0) & (beyond < chosen(plan, c, 2)))
        def _():
            for copy in copies(term, slot):
                copy.start()

        return tuple(seen + (c == number).astype(jnp.int32) for number, seen in enumerate(ranks))

    lax.fori_loop(0, terms, step, (jnp.int32(0),) * CLASSES)
    total = jnp.int32(0)
    for entries in plan:
        total += entries[2]

    @pl.loop(0, total)
    def _(slot):
        for copy in copies(0, slot):
            copy.wait()


def call_pack(shift, meta, left, right, ways, tick):
    smem, vmem = pl.BlockSpec(memory_space=pltpu.SMEM), pl.BlockSpec(memory_space=pltpu.VMEM)
    return pl.pallas_call(
        functools.partial(pack_terms, SPARE, ways),
        out_shape=[jax.ShapeDtypeStruct((SPARE, *array.shape[2:]), array.dtype) for array in (left, right)],
        in_specs=[smem, smem] + [pl.BlockSpec(memory_space=pl.ANY)] * 3,
        out_specs=[vmem, vmem],
        scratch_shapes=[pltpu.SemaphoreType.DMA((SPARE,)), pltpu.SemaphoreType.DMA((SPARE,))],
        compiler_params=pltpu.CompilerParams(vmem_limit_bytes=WHOLE_VMEM),
        cost_estimate=HINT,
    )(shift, meta, left, right, tick)


def sum_terms(kinds, ways, slots, pieces, outs, extras, ticks, resume, finish, mask, group, shift_ref, meta_ref, *refs):
    kind_parts = []
    for _ in kinds:
        kind_parts.append(refs[: ways * pieces])
        refs = refs[ways * pieces :]
    left_ref, right_ref, refs = refs[0], refs[1], refs[2:]
    if extras:
        extra_left_ref, extra_right_ref, refs = refs[0], refs[1], refs[2:]
    refs = refs[ticks:]
    if resume:
        before_ref, refs = refs[0], refs[1:]
    if finish:
        keep_ref, give_refs, refs = refs[0], refs[1:ways], refs[ways:]
    else:
        out_refs, refs = refs[:outs], refs[outs:]
    token_ref, left_buf, right_buf, source, applied, refs = *refs[:5], refs[5:]
    if finish or outs > 1:
        total, refs = refs[0], refs[1:]
    else:
        total = out_refs[0]
    left_sem, right_sem, part_sem, before_sem = refs
    place = meta_ref[PLACE]
    vectors = source.shape[1]
    _, share, columns = kind_parts[0][0].shape
    rows = share * ways
    widths = [kind_parts[0][piece * ways].shape[0] for piece in range(pieces)]

    def copy_parts(kind):
        for piece, width in enumerate(widths):
            for turn in range(ways):
                row = pl.multiple_of(lax.rem(place + ways - turn, ways) * share, share)
                yield pltpu.make_async_copy(
                    kind_parts[kind][piece * ways + turn],
                    source.at[kind, pl.ds(sum(widths[:piece]), width), pl.ds(row, share), :],
                    part_sem.at[kind, piece * ways + turn],
                )

    def copies(term, slot, lefts=left_ref.at[0], rights=right_ref.at[0]):
        return (
            pltpu.make_async_copy(lefts.at[term], left_buf.at[slot], left_sem.at[slot]),
            pltpu.make_async_copy(rights.at[term], right_buf.at[slot], right_sem.at[slot]),
        )

    for copy in copy_parts(0):
        copy.start()
    plan = sharing(shift_ref, meta_ref, shift_ref.shape[0], ways, SPARE) if extras else None
    counts = []
    for kind, position in enumerate(kinds):
        shift_class = jnp.int32(0) if position is None else meta_ref[position]
        kept = jnp.minimum(chosen(plan, shift_class, 0), slots) if extras else slots

        def fetch(term, count):
            hit = (shift_ref[term] == shift_class) & (count < kept)

            @pl.when(hit)
            def _():
                for copy in copies(term, kind * slots + count):
                    copy.start()

            return count + hit.astype(jnp.int32)

        count = lax.fori_loop(0, shift_ref.shape[0], fetch, jnp.int32(0))
        if extras:
            first = chosen(plan, shift_class, 3)
            more = jnp.minimum(chosen(plan, shift_class, 4), slots - count)

            @pl.loop(0, more)
            def _(turn):
                for copy in copies(first + turn, kind * slots + count + turn, extra_left_ref, extra_right_ref):
                    copy.start()

            count = count + more
        counts.append(count)
        if kind == 0:
            if resume:
                copy_before = pltpu.make_async_copy(before_ref, total, before_sem)
                copy_before.start()
            for later in range(1, len(kinds)):
                for copy in copy_parts(later):
                    copy.start()

    token_ref[...] = jnp.zeros_like(token_ref)
    if resume:
        copy_before.wait()
    else:
        total[...] = jnp.zeros_like(total)

    def arrive(slot):
        for copy in copies(0, slot):
            copy.wait()

    def add_terms(kind, first, number):
        rights = jnp.concatenate([right_buf[first + i] for i in range(number)], axis=1)
        for vector in range(vectors):
            for i in range(number):
                applied[vector, :, i * columns : (i + 1) * columns] = jnp.dot(
                    left_buf[first + i], source[kind, vector], preferred_element_type=jnp.float32
                ).astype(jnp.bfloat16)
        width = number * columns
        total[...] += lax.dot_general(
            applied[:, :, :width].reshape(vectors * rows, width),
            rights,
            (((1,), (1,)), ((), ())),
            preferred_element_type=jnp.float32,
        ).reshape(total.shape)

    for kind in range(len(kinds)):
        for copy in copy_parts(kind):
            copy.wait()
        if mask:
            kept_rows = lax.broadcasted_iota(jnp.int32, (rows, columns), 0) < meta_ref[LEFT]
            kept_block = kept_rows & (lax.broadcasted_iota(jnp.int32, (rows, columns), 1) < meta_ref[RIGHT])
            for vector in range(vectors):
                block = source[kind, vector]
                source[kind, vector] = jnp.where(kept_block, block, jnp.zeros_like(block))
        base = kind * slots
        whole = counts[kind] // group

        @pl.loop(0, whole)
        def _(turn):
            for i in range(group):
                arrive(base + turn * group + i)
            add_terms(kind, base + turn * group, group)

        if group > 1:

            @pl.loop(whole * group, counts[kind])
            def _(slot):
                arrive(base + slot)
                add_terms(kind, base + slot, 1)

    if finish:
        for turn in range(ways):
            row = pl.multiple_of(lax.rem(place + turn, ways) * share, share)
            block = total[:, pl.ds(row, share), :]
            if turn == 0:
                keep_ref[...] = block
            else:
                give_refs[turn - 1][...] = block.astype(jnp.bfloat16)
    elif outs > 1:
        for number, out_ref in enumerate(out_refs):
            begin = sum(out.shape[0] for out in out_refs[:number])
            out_ref[...] = total[pl.ds(begin, out_ref.shape[0])]


def call_terms(shift, meta, kinds, sources, left, right, extras=(), ticks=(), before=None, finish=False, mask=False, split=None):
    ways = len(sources[0][0])
    _, share, columns = sources[0][0][0].shape
    vectors = sum(parts[0].shape[0] for parts in sources[0])
    split = split or [vectors]
    rows = share * ways
    terms = left.shape[1]
    slots = min(terms, terms * ways // CLASSES)
    group = 1 if vectors >= 4 else 2
    any_spec = pl.BlockSpec(memory_space=pl.ANY)
    smem = pl.BlockSpec(memory_space=pltpu.SMEM)
    vmem = pl.BlockSpec(memory_space=pltpu.VMEM)
    parts = [part for pieces in sources for run in pieces for part in run]
    operands = [shift, meta, *parts, left, right, *extras, *ticks]
    if before is not None:
        operands.append(before)
    scratch = [
        pltpu.VMEM((len(kinds) * slots, rows, rows), jnp.bfloat16),
        pltpu.VMEM((len(kinds) * slots, columns, columns), jnp.bfloat16),
        pltpu.VMEM((len(kinds), vectors, rows, columns), jnp.bfloat16),
        pltpu.VMEM((vectors, rows, group * columns), jnp.bfloat16),
    ]
    if finish:
        out_shape = [jax.ShapeDtypeStruct((vectors, share, columns), jnp.float32)] + [
            jax.ShapeDtypeStruct((vectors, share, columns), jnp.bfloat16)
        ] * (ways - 1)
    else:
        out_shape = [jax.ShapeDtypeStruct((width, rows, columns), jnp.float32) for width in split]
    out_shape.append(jax.ShapeDtypeStruct((8, 128), jnp.int32))
    if finish or len(split) > 1:
        scratch.append(pltpu.VMEM((vectors, rows, columns), jnp.float32))
    scratch += [
        pltpu.SemaphoreType.DMA((len(kinds) * slots,)),
        pltpu.SemaphoreType.DMA((len(kinds) * slots,)),
        pltpu.SemaphoreType.DMA((len(kinds), ways * len(sources[0]))),
        pltpu.SemaphoreType.DMA,
    ]
    return pl.pallas_call(
        functools.partial(
            sum_terms, kinds, ways, slots, len(sources[0]), len(split), bool(extras), len(ticks),
            before is not None, finish, mask, group,
        ),
        out_shape=out_shape,
        in_specs=[smem, smem] + [any_spec] * (len(operands) - 2),
        out_specs=[vmem] * len(out_shape),
        scratch_shapes=scratch,
        compiler_params=pltpu.CompilerParams(vmem_limit_bytes=WHOLE_VMEM if mask else VMEM),
        cost_estimate=HINT,
    )(*operands)


def mask_rows(starts, meta_ref, source_ref, *refs):
    outs, (buffer, sem) = refs[:-2], refs[-2:]
    share, columns = source_ref.shape[2:]
    copy = pltpu.make_async_copy(source_ref.at[0], buffer, sem)
    copy.start()
    copy.wait()
    row = meta_ref[PLACE] * share + lax.broadcasted_iota(jnp.int32, (share, columns), 0)
    kept = (row < meta_ref[LEFT]) & (lax.broadcasted_iota(jnp.int32, (share, columns), 1) < meta_ref[RIGHT])
    for start, out in zip(starts, outs):
        for vector in range(out.shape[0]):
            block = buffer[start + vector]
            out[vector] = jnp.where(kept, block, jnp.zeros_like(block))


def call_mask(meta, wavefunction, starts, widths):
    share, columns = wavefunction.shape[2:]
    return pl.pallas_call(
        functools.partial(mask_rows, starts),
        out_shape=[jax.ShapeDtypeStruct((width, share, columns), wavefunction.dtype) for width in widths],
        in_specs=[pl.BlockSpec(memory_space=pltpu.SMEM), pl.BlockSpec(memory_space=pl.ANY)],
        out_specs=[pl.BlockSpec(memory_space=pltpu.VMEM)] * len(widths),
        scratch_shapes=[pltpu.VMEM(wavefunction.shape[1:], wavefunction.dtype), pltpu.SemaphoreType.DMA],
        compiler_params=pltpu.CompilerParams(vmem_limit_bytes=VMEM),
        cost_estimate=HINT,
    )(meta, wavefunction)


def permute(array, axis, pairs):
    return lax.ppermute(array, axis, sorted(pairs)) if pairs else jnp.zeros_like(array)


def around(array):
    ways = lax.axis_size("mpo")
    return [array] + [
        permute(array, "mpo", [(i, (i + turn) % ways) for i in range(ways)]) for turn in range(1, ways)
    ]


def after(array, tick):
    return lax.optimization_barrier((array, tick))


def per_device(wavefunction, left_env, right_env, left_dims, right_dims, term_shift):
    vectors, share, columns = wavefunction.shape[1:]
    place = lax.axis_index("mpo")
    ways = lax.axis_size("mpo")
    sector = lax.axis_index("sec")
    lines = lax.axis_size("sec") // SPINS
    line, spin = sector // SPINS, sector % SPINS
    odd = spin % 2 == 1
    row_ids = place * share + jnp.arange(share, dtype=jnp.int32)
    column_ids = jnp.arange(columns, dtype=jnp.int32)
    keep_mask = ((row_ids[:, None] < left_dims[0]) & (column_ids[None, :] < right_dims[0]))[None]

    def cross(step):
        return [
            (n * SPINS + p, (n + step) * SPINS + (p ^ 1))
            for n in range(lines)
            for p in range(SPINS)
            if 0 <= n + step < lines
        ]

    relay = [
        (n * SPINS + p, n * SPINS + p + (-2 if p % 2 else 2))
        for n in range(lines)
        for p in range(SPINS)
        if 0 <= p + (-2 if p % 2 else 2) < SPINS
    ]
    relay_here = jnp.where(odd, spin + 2 < SPINS, spin >= 2)
    from_below = (jnp.where(odd, 1, 3), jnp.where(odd, 3, 1), line > 0)
    from_above = (jnp.where(odd, 4, 2), jnp.where(odd, 2, 4), line + 1 < lines)
    if lines == 2:
        ways_across = [(cross(1) + cross(-1), tuple(jnp.where(line == 1, b, a) for b, a in zip(from_below, from_above)))]
    else:
        ways_across = [(cross(1), from_below), (cross(-1), from_above)] if lines > 1 else []
    classes = []
    for _, (near_class, far_class, valid) in ways_across:
        classes += [jnp.where(valid, near_class, -1), jnp.where(valid & relay_here, far_class, -1)]
    live_classes = [
        functools.reduce(jnp.logical_or, [found == c for found in classes], jnp.bool_(c == 0)) for c in range(CLASSES)
    ]
    meta = jnp.stack([place, left_dims[0], right_dims[0], *live_classes, *classes]).astype(jnp.int32)
    terms = functools.partial(call_terms, term_shift, meta)

    eighth = vectors // 8
    widths = [part * eighth for part in RUNS] if vectors % 8 == 0 else [vectors]
    starts = [sum(widths[:i]) for i in range(len(widths))]
    last = len(widths) - 1
    live = call_mask(meta, wavefunction, starts, widths)
    extras = ()
    if ways == 2 and SPARE:
        packed = call_pack(term_shift, meta, left_env, right_env, ways, live[-1])
        extras = [permute(part, "mpo", [(0, 1), (1, 0)]) for part in packed]
    landed, relayed, near, far, held = {}, {}, {}, {}, {}

    def send(index, tick=None):
        block = live[index]
        if tick is not None:
            block, tick = after(block, tick)
            held.setdefault((index, 0), []).append(tick)
        landed[index] = [permute(block, "sec", pairs) for pairs, _ in ways_across]

    def receive(index, tick):
        near[index], relayed[index] = [], []
        for block in landed[index]:
            block, passed = after(block, tick)
            held.setdefault((index, 0), []).append(passed)
            near[index].append(around(block))
            relayed[index].append(permute(block, "sec", relay))

    def share_far(index, tick=None):
        far[index] = []
        for part in relayed[index]:
            if tick is not None:
                part, passed = after(part, tick)
                held.setdefault((index, 1), []).append(passed)
            far[index].append(around(part))

    def add(members, total, positions, ticks):
        ticks = list(ticks)
        for way in range(len(ways_across)):
            kinds = [OWN + 2 * way + position for position in positions]
            sources = [[(far if position else near)[index][way] for index in members] for position in positions]
            waits = ticks + [t for position in positions for index in members for t in held.get((index, position), [])]
            finish = 1 in positions and way == len(ways_across) - 1
            *total, tick = terms(kinds, sources, left_env, right_env, extras, waits, total, finish=finish)
            ticks = [tick]
            if not finish:
                total = total[0]
        return total, ticks[0]

    send(0)
    *totals, tick = terms([None], [[around(wavefunction[0])]], left_env, right_env, extras, mask=True, split=widths)
    if last:
        send(1, tick)
    if ways_across:
        receive(0, tick)
        for index in range(last + 1):
            if index == last and index > 1:
                share_far(index, tick)
                totals[index], tick = add([index], totals[index], (0, 1), [tick])
                continue
            total, tick = add([index], totals[index], (0,), [tick])
            share_far(index, tick)
            if index + 1 <= last:
                receive(index + 1, tick)
            if index + 2 <= last:
                send(index + 2, tick)
            totals[index], tick = add([index], total, (1,), [tick])

    blocks = []
    for index in range(last + 1):
        sums, *gifts = totals[index] if ways_across else (totals[index][:, :share],)
        for turn, given in enumerate(gifts, 1):
            sums += permute(given, "mpo", [(i, (i + turn) % ways) for i in range(ways)]).astype(jnp.float32)
        blocks.append(jnp.where(keep_mask, sums, jnp.zeros_like(sums)).astype(jnp.bfloat16))
    return jnp.concatenate(blocks)[None]


def solution(mesh):
    in_specs = (
        P("sec", None, "mpo", None),
        P("sec", "mpo", None, None),
        P("sec", "mpo", None, None),
        P("sec"),
        P("sec"),
        P("mpo"),
    )
    out_specs = P("sec", None, "mpo", None)
    return jax.shard_map(
        per_device, mesh=mesh, in_specs=in_specs, out_specs=out_specs, check_vma=False
    )
```

```python
import functools

import jax
import jax.numpy as jnp
from jax import lax
from jax.experimental import pallas as pl
from jax.experimental.pallas import tpu as pltpu
from jax.sharding import PartitionSpec as P

SPINS = 8
CLASSES = 5
SPARE = 0
VMEM = 40 * 2**20
WHOLE_VMEM = 62 * 2**20
RUNS = (3, 5)
PLACE, LEFT, RIGHT, LIVE, OWN = 0, 1, 2, 3, 3 + CLASSES
HINT = pl.CostEstimate(flops=10**6, bytes_accessed=10**3, transcendentals=0)


def sharing(shift_ref, meta_ref, terms, ways, spare):
    both = terms * ways // CLASSES
    half = both // 2

    def tally(term, counts):
        return tuple(n + (shift_ref[term] == c).astype(jnp.int32) for c, n in enumerate(counts))

    counts = lax.fori_loop(0, terms, tally, (jnp.int32(0),) * CLASSES)
    given_before, taken_before, plan = jnp.int32(0), jnp.int32(0), []
    for c, count in enumerate(counts):
        live = meta_ref[LIVE + c]
        surplus = jnp.maximum(count - half, 0) * live
        lack = jnp.maximum(both - half - (count if both % 2 == 0 else count), 0) * live
        given = jnp.clip(spare - given_before, 0, surplus)
        taken = jnp.clip(spare - taken_before, 0, lack)
        plan.append((count - given, given_before, given, taken_before, taken))
        given_before, taken_before = given_before + surplus, taken_before + lack
    return plan


def chosen(plan, shift_class, entry):
    value = jnp.int32(0)
    for c, entries in enumerate(plan):
        value = jnp.where(shift_class == c, entries[entry], value)
    return value


def pack_terms(spare, ways, shift_ref, meta_ref, left_ref, right_ref, _, lefts, rights, left_sem, right_sem):
    terms = shift_ref.shape[0]
    plan = sharing(shift_ref, meta_ref, terms, ways, spare)

    def copies(term, slot):
        return (
            pltpu.make_async_copy(left_ref.at[0, term], lefts.at[slot], left_sem.at[slot]),
            pltpu.make_async_copy(right_ref.at[0, term], rights.at[slot], right_sem.at[slot]),
        )

    def step(term, ranks):
        c = shift_ref[term]
        rank = jnp.int32(0)
        for number, seen in enumerate(ranks):
            rank = jnp.where(c == number, seen, rank)
        beyond = rank - chosen(plan, c, 0)
        slot = chosen(plan, c, 1) + beyond

        @pl.when((beyond >= 0) & (beyond < chosen(plan, c, 2)))
        def _():
            for copy in copies(term, slot):
                copy.start()

        return tuple(seen + (c == number).astype(jnp.int32) for number, seen in enumerate(ranks))

    lax.fori_loop(0, terms, step, (jnp.int32(0),) * CLASSES)
    total = jnp.int32(0)
    for entries in plan:
        total += entries[2]

    @pl.loop(0, total)
    def _(slot):
        for copy in copies(0, slot):
            copy.wait()


def call_pack(shift, meta, left, right, ways, tick):
    smem, vmem = pl.BlockSpec(memory_space=pltpu.SMEM), pl.BlockSpec(memory_space=pltpu.VMEM)
    return pl.pallas_call(
        functools.partial(pack_terms, SPARE, ways),
        out_shape=[jax.ShapeDtypeStruct((SPARE, *array.shape[2:]), array.dtype) for array in (left, right)],
        in_specs=[smem, smem] + [pl.BlockSpec(memory_space=pl.ANY)] * 3,
        out_specs=[vmem, vmem],
        scratch_shapes=[pltpu.SemaphoreType.DMA((SPARE,)), pltpu.SemaphoreType.DMA((SPARE,))],
        compiler_params=pltpu.CompilerParams(vmem_limit_bytes=WHOLE_VMEM),
        cost_estimate=HINT,
    )(shift, meta, left, right, tick)


def sum_terms(kinds, ways, slots, pieces, outs, extras, ticks, resume, finish, mask, group, shift_ref, meta_ref, *refs):
    kind_parts = []
    for _ in kinds:
        kind_parts.append(refs[: ways * pieces])
        refs = refs[ways * pieces :]
    left_ref, right_ref, refs = refs[0], refs[1], refs[2:]
    if extras:
        extra_left_ref, extra_right_ref, refs = refs[0], refs[1], refs[2:]
    refs = refs[ticks:]
    if resume:
        before_ref, refs = refs[0], refs[1:]
    if finish:
        keep_ref, give_refs, refs = refs[0], refs[1:ways], refs[ways:]
    else:
        out_refs, refs = refs[:outs], refs[outs:]
    token_ref, left_buf, right_buf, source, applied, refs = *refs[:5], refs[5:]
    if finish or outs > 1:
        total, refs = refs[0], refs[1:]
    else:
        total = out_refs[0]
    left_sem, right_sem, part_sem, before_sem = refs
    place = meta_ref[PLACE]
    vectors = source.shape[1]
    _, share, columns = kind_parts[0][0].shape
    rows = share * ways
    widths = [kind_parts[0][piece * ways].shape[0] for piece in range(pieces)]

    def copy_parts(kind):
        for piece, width in enumerate(widths):
            for turn in range(ways):
                row = pl.multiple_of(lax.rem(place + ways - turn, ways) * share, share)
                yield pltpu.make_async_copy(
                    kind_parts[kind][piece * ways + turn],
                    source.at[kind, pl.ds(sum(widths[:piece]), width), pl.ds(row, share), :],
                    part_sem.at[kind, piece * ways + turn],
                )

    def copies(term, slot, lefts=left_ref.at[0], rights=right_ref.at[0]):
        return (
            pltpu.make_async_copy(lefts.at[term], left_buf.at[slot], left_sem.at[slot]),
            pltpu.make_async_copy(rights.at[term], right_buf.at[slot], right_sem.at[slot]),
        )

    for copy in copy_parts(0):
        copy.start()
    plan = sharing(shift_ref, meta_ref, shift_ref.shape[0], ways, SPARE) if extras else None
    counts = []
    for kind, position in enumerate(kinds):
        shift_class = jnp.int32(0) if position is None else meta_ref[position]
        kept = jnp.minimum(chosen(plan, shift_class, 0), slots) if extras else slots

        def fetch(term, count):
            hit = (shift_ref[term] == shift_class) & (count < kept)

            @pl.when(hit)
            def _():
                for copy in copies(term, kind * slots + count):
                    copy.start()

            return count + hit.astype(jnp.int32)

        count = lax.fori_loop(0, shift_ref.shape[0], fetch, jnp.int32(0))
        if extras:
            first = chosen(plan, shift_class, 3)
            more = jnp.minimum(chosen(plan, shift_class, 4), slots - count)

            @pl.loop(0, more)
            def _(turn):
                for copy in copies(first + turn, kind * slots + count + turn, extra_left_ref, extra_right_ref):
                    copy.start()

            count = count + more
        counts.append(count)
        if kind == 0:
            if resume:
                copy_before = pltpu.make_async_copy(before_ref, total, before_sem)
                copy_before.start()
            for later in range(1, len(kinds)):
                for copy in copy_parts(later):
                    copy.start()

    token_ref[...] = jnp.zeros_like(token_ref)
    if resume:
        copy_before.wait()
    else:
        total[...] = jnp.zeros_like(total)

    def arrive(slot):
        for copy in copies(0, slot):
            copy.wait()

    def add_terms(kind, first, number):
        rights = jnp.concatenate([right_buf[first + i] for i in range(number)], axis=1)
        for vector in range(vectors):
            for i in range(number):
                applied[vector, :, i * columns : (i + 1) * columns] = jnp.dot(
                    left_buf[first + i], source[kind, vector], preferred_element_type=jnp.float32
                ).astype(jnp.bfloat16)
        width = number * columns
        total[...] += lax.dot_general(
            applied[:, :, :width].reshape(vectors * rows, width),
            rights,
            (((1,), (1,)), ((), ())),
            preferred_element_type=jnp.float32,
        ).reshape(total.shape)

    for kind in range(len(kinds)):
        for copy in copy_parts(kind):
            copy.wait()
        if mask:
            kept_rows = lax.broadcasted_iota(jnp.int32, (rows, columns), 0) < meta_ref[LEFT]
            kept_block = kept_rows & (lax.broadcasted_iota(jnp.int32, (rows, columns), 1) < meta_ref[RIGHT])
            for vector in range(vectors):
                block = source[kind, vector]
                source[kind, vector] = jnp.where(kept_block, block, jnp.zeros_like(block))
        base = kind * slots
        whole = counts[kind] // group

        @pl.loop(0, whole)
        def _(turn):
            for i in range(group):
                arrive(base + turn * group + i)
            add_terms(kind, base + turn * group, group)

        if group > 1:

            @pl.loop(whole * group, counts[kind])
            def _(slot):
                arrive(base + slot)
                add_terms(kind, base + slot, 1)

    if finish:
        for turn in range(ways):
            row = pl.multiple_of(lax.rem(place + turn, ways) * share, share)
            block = total[:, pl.ds(row, share), :]
            if turn == 0:
                keep_ref[...] = block
            else:
                give_refs[turn - 1][...] = block.astype(jnp.bfloat16)
    elif outs > 1:
        for number, out_ref in enumerate(out_refs):
            begin = sum(out.shape[0] for out in out_refs[:number])
            out_ref[...] = total[pl.ds(begin, out_ref.shape[0])]


def call_terms(shift, meta, kinds, sources, left, right, extras=(), ticks=(), before=None, finish=False, mask=False, split=None):
    ways = len(sources[0][0])
    _, share, columns = sources[0][0][0].shape
    vectors = sum(parts[0].shape[0] for parts in sources[0])
    split = split or [vectors]
    rows = share * ways
    terms = left.shape[1]
    slots = min(terms, terms * ways // CLASSES)
    group = 1 if vectors >= 4 else 2
    any_spec = pl.BlockSpec(memory_space=pl.ANY)
    smem = pl.BlockSpec(memory_space=pltpu.SMEM)
    vmem = pl.BlockSpec(memory_space=pltpu.VMEM)
    parts = [part for pieces in sources for run in pieces for part in run]
    operands = [shift, meta, *parts, left, right, *extras, *ticks]
    if before is not None:
        operands.append(before)
    scratch = [
        pltpu.VMEM((len(kinds) * slots, rows, rows), jnp.bfloat16),
        pltpu.VMEM((len(kinds) * slots, columns, columns), jnp.bfloat16),
        pltpu.VMEM((len(kinds), vectors, rows, columns), jnp.bfloat16),
        pltpu.VMEM((vectors, rows, group * columns), jnp.bfloat16),
    ]
    if finish:
        out_shape = [jax.ShapeDtypeStruct((vectors, share, columns), jnp.float32)] + [
            jax.ShapeDtypeStruct((vectors, share, columns), jnp.bfloat16)
        ] * (ways - 1)
    else:
        out_shape = [jax.ShapeDtypeStruct((width, rows, columns), jnp.float32) for width in split]
    out_shape.append(jax.ShapeDtypeStruct((8, 128), jnp.int32))
    if finish or len(split) > 1:
        scratch.append(pltpu.VMEM((vectors, rows, columns), jnp.float32))
    scratch += [
        pltpu.SemaphoreType.DMA((len(kinds) * slots,)),
        pltpu.SemaphoreType.DMA((len(kinds) * slots,)),
        pltpu.SemaphoreType.DMA((len(kinds), ways * len(sources[0]))),
        pltpu.SemaphoreType.DMA,
    ]
    return pl.pallas_call(
        functools.partial(
            sum_terms, kinds, ways, slots, len(sources[0]), len(split), bool(extras), len(ticks),
            before is not None, finish, mask, group,
        ),
        out_shape=out_shape,
        in_specs=[smem, smem] + [any_spec] * (len(operands) - 2),
        out_specs=[vmem] * len(out_shape),
        scratch_shapes=scratch,
        compiler_params=pltpu.CompilerParams(vmem_limit_bytes=WHOLE_VMEM if mask else VMEM),
        cost_estimate=HINT,
    )(*operands)


def mask_rows(starts, meta_ref, source_ref, *refs):
    outs, (buffer, sem) = refs[:-2], refs[-2:]
    share, columns = source_ref.shape[2:]
    copy = pltpu.make_async_copy(source_ref.at[0], buffer, sem)
    copy.start()
    copy.wait()
    row = meta_ref[PLACE] * share + lax.broadcasted_iota(jnp.int32, (share, columns), 0)
    kept = (row < meta_ref[LEFT]) & (lax.broadcasted_iota(jnp.int32, (share, columns), 1) < meta_ref[RIGHT])
    for start, out in zip(starts, outs):
        for vector in range(out.shape[0]):
            block = buffer[start + vector]
            out[vector] = jnp.where(kept, block, jnp.zeros_like(block))


def call_mask(meta, wavefunction, starts, widths):
    share, columns = wavefunction.shape[2:]
    return pl.pallas_call(
        functools.partial(mask_rows, starts),
        out_shape=[jax.ShapeDtypeStruct((width, share, columns), wavefunction.dtype) for width in widths],
        in_specs=[pl.BlockSpec(memory_space=pltpu.SMEM), pl.BlockSpec(memory_space=pl.ANY)],
        out_specs=[pl.BlockSpec(memory_space=pltpu.VMEM)] * len(widths),
        scratch_shapes=[pltpu.VMEM(wavefunction.shape[1:], wavefunction.dtype), pltpu.SemaphoreType.DMA],
        compiler_params=pltpu.CompilerParams(vmem_limit_bytes=VMEM),
        cost_estimate=HINT,
    )(meta, wavefunction)


def permute(array, axis, pairs):
    return lax.ppermute(array, axis, sorted(pairs)) if pairs else jnp.zeros_like(array)


def around(array):
    ways = lax.axis_size("mpo")
    return [array] + [
        permute(array, "mpo", [(i, (i + turn) % ways) for i in range(ways)]) for turn in range(1, ways)
    ]


def after(array, tick):
    return lax.optimization_barrier((array, tick))


def per_device(wavefunction, left_env, right_env, left_dims, right_dims, term_shift):
    vectors, share, columns = wavefunction.shape[1:]
    place = lax.axis_index("mpo")
    ways = lax.axis_size("mpo")
    sector = lax.axis_index("sec")
    lines = lax.axis_size("sec") // SPINS
    line, spin = sector // SPINS, sector % SPINS
    odd = spin % 2 == 1
    row_ids = place * share + jnp.arange(share, dtype=jnp.int32)
    column_ids = jnp.arange(columns, dtype=jnp.int32)
    keep_mask = ((row_ids[:, None] < left_dims[0]) & (column_ids[None, :] < right_dims[0]))[None]

    def cross(step):
        return [
            (n * SPINS + p, (n + step) * SPINS + (p ^ 1))
            for n in range(lines)
            for p in range(SPINS)
            if 0 <= n + step < lines
        ]

    relay = [
        (n * SPINS + p, n * SPINS + p + (-2 if p % 2 else 2))
        for n in range(lines)
        for p in range(SPINS)
        if 0 <= p + (-2 if p % 2 else 2) < SPINS
    ]
    relay_here = jnp.where(odd, spin + 2 < SPINS, spin >= 2)
    from_below = (jnp.where(odd, 1, 3), jnp.where(odd, 3, 1), line > 0)
    from_above = (jnp.where(odd, 4, 2), jnp.where(odd, 2, 4), line + 1 < lines)
    if lines == 2:
        ways_across = [(cross(1) + cross(-1), tuple(jnp.where(line == 1, b, a) for b, a in zip(from_below, from_above)))]
    else:
        ways_across = [(cross(1), from_below), (cross(-1), from_above)] if lines > 1 else []
    classes = []
    for _, (near_class, far_class, valid) in ways_across:
        classes += [jnp.where(valid, near_class, -1), jnp.where(valid & relay_here, far_class, -1)]
    live_classes = [
        functools.reduce(jnp.logical_or, [found == c for found in classes], jnp.bool_(c == 0)) for c in range(CLASSES)
    ]
    meta = jnp.stack([place, left_dims[0], right_dims[0], *live_classes, *classes]).astype(jnp.int32)
    terms = functools.partial(call_terms, term_shift, meta)

    eighth = vectors // 8
    widths = [part * eighth for part in RUNS] if vectors % 8 == 0 else [vectors]
    starts = [sum(widths[:i]) for i in range(len(widths))]
    last = len(widths) - 1
    live = call_mask(meta, wavefunction, starts, widths)
    extras = ()
    if ways == 2 and SPARE:
        packed = call_pack(term_shift, meta, left_env, right_env, ways, live[-1])
        extras = [permute(part, "mpo", [(0, 1), (1, 0)]) for part in packed]
    landed, relayed, near, far, held = {}, {}, {}, {}, {}

    def send(index, tick=None):
        block = live[index]
        if tick is not None:
            block, tick = after(block, tick)
            held.setdefault((index, 0), []).append(tick)
        landed[index] = [permute(block, "sec", pairs) for pairs, _ in ways_across]

    def receive(index, tick):
        near[index], relayed[index] = [], []
        for block in landed[index]:
            block, passed = after(block, tick)
            held.setdefault((index, 0), []).append(passed)
            near[index].append(around(block))
            relayed[index].append(permute(block, "sec", relay))

    def share_far(index, tick=None):
        far[index] = []
        for part in relayed[index]:
            if tick is not None:
                part, passed = after(part, tick)
                held.setdefault((index, 1), []).append(passed)
            far[index].append(around(part))

    def add(members, total, positions, ticks):
        ticks = list(ticks)
        for way in range(len(ways_across)):
            kinds = [OWN + 2 * way + position for position in positions]
            sources = [[(far if position else near)[index][way] for index in members] for position in positions]
            waits = ticks + [t for position in positions for index in members for t in held.get((index, position), [])]
            finish = 1 in positions and way == len(ways_across) - 1
            *total, tick = terms(kinds, sources, left_env, right_env, extras, waits, total, finish=finish)
            ticks = [tick]
            if not finish:
                total = total[0]
        return total, ticks[0]

    send(0)
    *totals, tick = terms([None], [[around(wavefunction[0])]], left_env, right_env, extras, mask=True, split=widths)
    if last:
        send(1, tick)
    if ways_across:
        receive(0, tick)
        for index in range(last + 1):
            if index == last and index > 1:
                share_far(index, tick)
                totals[index], tick = add([index], totals[index], (0, 1), [tick])
                continue
            total, tick = add([index], totals[index], (0,), [tick])
            share_far(index, tick)
            if index + 1 <= last:
                receive(index + 1, tick)
            if index + 2 <= last:
                send(index + 2, tick)
            totals[index], tick = add([index], total, (1,), [tick])

    blocks = []
    for index in range(last + 1):
        sums, *gifts = totals[index] if ways_across else (totals[index][:, :share],)
        for turn, given in enumerate(gifts, 1):
            sums += permute(given, "mpo", [(i, (i + turn) % ways) for i in range(ways)]).astype(jnp.float32)
        blocks.append(jnp.where(keep_mask, sums, jnp.zeros_like(sums)).astype(jnp.bfloat16))
    return jnp.concatenate(blocks)[None]


def solution(mesh):
    in_specs = (
        P("sec", None, "mpo", None),
        P("sec", "mpo", None, None),
        P("sec", "mpo", None, None),
        P("sec"),
        P("sec"),
        P("mpo"),
    )
    out_specs = P("sec", None, "mpo", None)
    return jax.shard_map(
        per_device, mesh=mesh, in_specs=in_specs, out_specs=out_specs, check_vma=False
    )
```

```python
import functools

import jax
import jax.numpy as jnp
from jax import lax
from jax.experimental import pallas as pl
from jax.experimental.pallas import tpu as pltpu
from jax.sharding import PartitionSpec as P

SPINS = 8
CLASSES = 5
SPARE = 0
VMEM = 40 * 2**20
WHOLE_VMEM = 62 * 2**20
RUNS = (3, 3, 2)
PLACE, LEFT, RIGHT, LIVE, OWN = 0, 1, 2, 3, 3 + CLASSES
HINT = pl.CostEstimate(flops=10**6, bytes_accessed=10**3, transcendentals=0)


def sharing(shift_ref, meta_ref, terms, ways, spare):
    both = terms * ways // CLASSES
    half = both // 2

    def tally(term, counts):
        return tuple(n + (shift_ref[term] == c).astype(jnp.int32) for c, n in enumerate(counts))

    counts = lax.fori_loop(0, terms, tally, (jnp.int32(0),) * CLASSES)
    given_before, taken_before, plan = jnp.int32(0), jnp.int32(0), []
    for c, count in enumerate(counts):
        live = meta_ref[LIVE + c]
        surplus = jnp.maximum(count - half, 0) * live
        lack = jnp.maximum(both - half - (count if both % 2 == 0 else count), 0) * live
        given = jnp.clip(spare - given_before, 0, surplus)
        taken = jnp.clip(spare - taken_before, 0, lack)
        plan.append((count - given, given_before, given, taken_before, taken))
        given_before, taken_before = given_before + surplus, taken_before + lack
    return plan


def chosen(plan, shift_class, entry):
    value = jnp.int32(0)
    for c, entries in enumerate(plan):
        value = jnp.where(shift_class == c, entries[entry], value)
    return value


def pack_terms(spare, ways, shift_ref, meta_ref, left_ref, right_ref, _, lefts, rights, left_sem, right_sem):
    terms = shift_ref.shape[0]
    plan = sharing(shift_ref, meta_ref, terms, ways, spare)

    def copies(term, slot):
        return (
            pltpu.make_async_copy(left_ref.at[0, term], lefts.at[slot], left_sem.at[slot]),
            pltpu.make_async_copy(right_ref.at[0, term], rights.at[slot], right_sem.at[slot]),
        )

    def step(term, ranks):
        c = shift_ref[term]
        rank = jnp.int32(0)
        for number, seen in enumerate(ranks):
            rank = jnp.where(c == number, seen, rank)
        beyond = rank - chosen(plan, c, 0)
        slot = chosen(plan, c, 1) + beyond

        @pl.when((beyond >= 0) & (beyond < chosen(plan, c, 2)))
        def _():
            for copy in copies(term, slot):
                copy.start()

        return tuple(seen + (c == number).astype(jnp.int32) for number, seen in enumerate(ranks))

    lax.fori_loop(0, terms, step, (jnp.int32(0),) * CLASSES)
    total = jnp.int32(0)
    for entries in plan:
        total += entries[2]

    @pl.loop(0, total)
    def _(slot):
        for copy in copies(0, slot):
            copy.wait()


def call_pack(shift, meta, left, right, ways, tick):
    smem, vmem = pl.BlockSpec(memory_space=pltpu.SMEM), pl.BlockSpec(memory_space=pltpu.VMEM)
    return pl.pallas_call(
        functools.partial(pack_terms, SPARE, ways),
        out_shape=[jax.ShapeDtypeStruct((SPARE, *array.shape[2:]), array.dtype) for array in (left, right)],
        in_specs=[smem, smem] + [pl.BlockSpec(memory_space=pl.ANY)] * 3,
        out_specs=[vmem, vmem],
        scratch_shapes=[pltpu.SemaphoreType.DMA((SPARE,)), pltpu.SemaphoreType.DMA((SPARE,))],
        compiler_params=pltpu.CompilerParams(vmem_limit_bytes=WHOLE_VMEM),
        cost_estimate=HINT,
    )(shift, meta, left, right, tick)


def sum_terms(kinds, ways, slots, pieces, outs, extras, ticks, resume, finish, mask, group, shift_ref, meta_ref, *refs):
    kind_parts = []
    for _ in kinds:
        kind_parts.append(refs[: ways * pieces])
        refs = refs[ways * pieces :]
    left_ref, right_ref, refs = refs[0], refs[1], refs[2:]
    if extras:
        extra_left_ref, extra_right_ref, refs = refs[0], refs[1], refs[2:]
    refs = refs[ticks:]
    if resume:
        before_ref, refs = refs[0], refs[1:]
    if finish:
        keep_ref, give_refs, refs = refs[0], refs[1:ways], refs[ways:]
    else:
        out_refs, refs = refs[:outs], refs[outs:]
    token_ref, left_buf, right_buf, source, applied, refs = *refs[:5], refs[5:]
    if finish or outs > 1:
        total, refs = refs[0], refs[1:]
    else:
        total = out_refs[0]
    left_sem, right_sem, part_sem, before_sem = refs
    place = meta_ref[PLACE]
    vectors = source.shape[1]
    _, share, columns = kind_parts[0][0].shape
    rows = share * ways
    widths = [kind_parts[0][piece * ways].shape[0] for piece in range(pieces)]

    def copy_parts(kind):
        for piece, width in enumerate(widths):
            for turn in range(ways):
                row = pl.multiple_of(lax.rem(place + ways - turn, ways) * share, share)
                yield pltpu.make_async_copy(
                    kind_parts[kind][piece * ways + turn],
                    source.at[kind, pl.ds(sum(widths[:piece]), width), pl.ds(row, share), :],
                    part_sem.at[kind, piece * ways + turn],
                )

    def copies(term, slot, lefts=left_ref.at[0], rights=right_ref.at[0]):
        return (
            pltpu.make_async_copy(lefts.at[term], left_buf.at[slot], left_sem.at[slot]),
            pltpu.make_async_copy(rights.at[term], right_buf.at[slot], right_sem.at[slot]),
        )

    for copy in copy_parts(0):
        copy.start()
    plan = sharing(shift_ref, meta_ref, shift_ref.shape[0], ways, SPARE) if extras else None
    counts = []
    for kind, position in enumerate(kinds):
        shift_class = jnp.int32(0) if position is None else meta_ref[position]
        kept = jnp.minimum(chosen(plan, shift_class, 0), slots) if extras else slots

        def fetch(term, count):
            hit = (shift_ref[term] == shift_class) & (count < kept)

            @pl.when(hit)
            def _():
                for copy in copies(term, kind * slots + count):
                    copy.start()

            return count + hit.astype(jnp.int32)

        count = lax.fori_loop(0, shift_ref.shape[0], fetch, jnp.int32(0))
        if extras:
            first = chosen(plan, shift_class, 3)
            more = jnp.minimum(chosen(plan, shift_class, 4), slots - count)

            @pl.loop(0, more)
            def _(turn):
                for copy in copies(first + turn, kind * slots + count + turn, extra_left_ref, extra_right_ref):
                    copy.start()

            count = count + more
        counts.append(count)
        if kind == 0:
            if resume:
                copy_before = pltpu.make_async_copy(before_ref, total, before_sem)
                copy_before.start()
            for later in range(1, len(kinds)):
                for copy in copy_parts(later):
                    copy.start()

    token_ref[...] = jnp.zeros_like(token_ref)
    if resume:
        copy_before.wait()
    else:
        total[...] = jnp.zeros_like(total)

    def arrive(slot):
        for copy in copies(0, slot):
            copy.wait()

    def add_terms(kind, first, number):
        rights = jnp.concatenate([right_buf[first + i] for i in range(number)], axis=1)
        for vector in range(vectors):
            for i in range(number):
                applied[vector, :, i * columns : (i + 1) * columns] = jnp.dot(
                    left_buf[first + i], source[kind, vector], preferred_element_type=jnp.float32
                ).astype(jnp.bfloat16)
        width = number * columns
        total[...] += lax.dot_general(
            applied[:, :, :width].reshape(vectors * rows, width),
            rights,
            (((1,), (1,)), ((), ())),
            preferred_element_type=jnp.float32,
        ).reshape(total.shape)

    for kind in range(len(kinds)):
        for copy in copy_parts(kind):
            copy.wait()
        if mask:
            kept_rows = lax.broadcasted_iota(jnp.int32, (rows, columns), 0) < meta_ref[LEFT]
            kept_block = kept_rows & (lax.broadcasted_iota(jnp.int32, (rows, columns), 1) < meta_ref[RIGHT])
            for vector in range(vectors):
                block = source[kind, vector]
                source[kind, vector] = jnp.where(kept_block, block, jnp.zeros_like(block))
        base = kind * slots
        whole = counts[kind] // group

        @pl.loop(0, whole)
        def _(turn):
            for i in range(group):
                arrive(base + turn * group + i)
            add_terms(kind, base + turn * group, group)

        if group > 1:

            @pl.loop(whole * group, counts[kind])
            def _(slot):
                arrive(base + slot)
                add_terms(kind, base + slot, 1)

    if finish:
        for turn in range(ways):
            row = pl.multiple_of(lax.rem(place + turn, ways) * share, share)
            block = total[:, pl.ds(row, share), :]
            if turn == 0:
                keep_ref[...] = block
            else:
                give_refs[turn - 1][...] = block.astype(jnp.bfloat16)
    elif outs > 1:
        for number, out_ref in enumerate(out_refs):
            begin = sum(out.shape[0] for out in out_refs[:number])
            out_ref[...] = total[pl.ds(begin, out_ref.shape[0])]


def call_terms(shift, meta, kinds, sources, left, right, extras=(), ticks=(), before=None, finish=False, mask=False, split=None):
    ways = len(sources[0][0])
    _, share, columns = sources[0][0][0].shape
    vectors = sum(parts[0].shape[0] for parts in sources[0])
    split = split or [vectors]
    rows = share * ways
    terms = left.shape[1]
    slots = min(terms, terms * ways // CLASSES)
    group = 1 if vectors >= 4 else 2
    any_spec = pl.BlockSpec(memory_space=pl.ANY)
    smem = pl.BlockSpec(memory_space=pltpu.SMEM)
    vmem = pl.BlockSpec(memory_space=pltpu.VMEM)
    parts = [part for pieces in sources for run in pieces for part in run]
    operands = [shift, meta, *parts, left, right, *extras, *ticks]
    if before is not None:
        operands.append(before)
    scratch = [
        pltpu.VMEM((len(kinds) * slots, rows, rows), jnp.bfloat16),
        pltpu.VMEM((len(kinds) * slots, columns, columns), jnp.bfloat16),
        pltpu.VMEM((len(kinds), vectors, rows, columns), jnp.bfloat16),
        pltpu.VMEM((vectors, rows, group * columns), jnp.bfloat16),
    ]
    if finish:
        out_shape = [jax.ShapeDtypeStruct((vectors, share, columns), jnp.float32)] + [
            jax.ShapeDtypeStruct((vectors, share, columns), jnp.bfloat16)
        ] * (ways - 1)
    else:
        out_shape = [jax.ShapeDtypeStruct((width, rows, columns), jnp.float32) for width in split]
    out_shape.append(jax.ShapeDtypeStruct((8, 128), jnp.int32))
    if finish or len(split) > 1:
        scratch.append(pltpu.VMEM((vectors, rows, columns), jnp.float32))
    scratch += [
        pltpu.SemaphoreType.DMA((len(kinds) * slots,)),
        pltpu.SemaphoreType.DMA((len(kinds) * slots,)),
        pltpu.SemaphoreType.DMA((len(kinds), ways * len(sources[0]))),
        pltpu.SemaphoreType.DMA,
    ]
    return pl.pallas_call(
        functools.partial(
            sum_terms, kinds, ways, slots, len(sources[0]), len(split), bool(extras), len(ticks),
            before is not None, finish, mask, group,
        ),
        out_shape=out_shape,
        in_specs=[smem, smem] + [any_spec] * (len(operands) - 2),
        out_specs=[vmem] * len(out_shape),
        scratch_shapes=scratch,
        compiler_params=pltpu.CompilerParams(vmem_limit_bytes=WHOLE_VMEM if mask else VMEM),
        cost_estimate=HINT,
    )(*operands)


def mask_rows(starts, meta_ref, source_ref, *refs):
    outs, (buffer, sem) = refs[:-2], refs[-2:]
    share, columns = source_ref.shape[2:]
    copy = pltpu.make_async_copy(source_ref.at[0], buffer, sem)
    copy.start()
    copy.wait()
    row = meta_ref[PLACE] * share + lax.broadcasted_iota(jnp.int32, (share, columns), 0)
    kept = (row < meta_ref[LEFT]) & (lax.broadcasted_iota(jnp.int32, (share, columns), 1) < meta_ref[RIGHT])
    for start, out in zip(starts, outs):
        for vector in range(out.shape[0]):
            block = buffer[start + vector]
            out[vector] = jnp.where(kept, block, jnp.zeros_like(block))


def call_mask(meta, wavefunction, starts, widths):
    share, columns = wavefunction.shape[2:]
    return pl.pallas_call(
        functools.partial(mask_rows, starts),
        out_shape=[jax.ShapeDtypeStruct((width, share, columns), wavefunction.dtype) for width in widths],
        in_specs=[pl.BlockSpec(memory_space=pltpu.SMEM), pl.BlockSpec(memory_space=pl.ANY)],
        out_specs=[pl.BlockSpec(memory_space=pltpu.VMEM)] * len(widths),
        scratch_shapes=[pltpu.VMEM(wavefunction.shape[1:], wavefunction.dtype), pltpu.SemaphoreType.DMA],
        compiler_params=pltpu.CompilerParams(vmem_limit_bytes=VMEM),
        cost_estimate=HINT,
    )(meta, wavefunction)


def permute(array, axis, pairs):
    return lax.ppermute(array, axis, sorted(pairs)) if pairs else jnp.zeros_like(array)


def around(array):
    ways = lax.axis_size("mpo")
    return [array] + [
        permute(array, "mpo", [(i, (i + turn) % ways) for i in range(ways)]) for turn in range(1, ways)
    ]


def after(array, tick):
    return lax.optimization_barrier((array, tick))


def per_device(wavefunction, left_env, right_env, left_dims, right_dims, term_shift):
    vectors, share, columns = wavefunction.shape[1:]
    place = lax.axis_index("mpo")
    ways = lax.axis_size("mpo")
    sector = lax.axis_index("sec")
    lines = lax.axis_size("sec") // SPINS
    line, spin = sector // SPINS, sector % SPINS
    odd = spin % 2 == 1
    row_ids = place * share + jnp.arange(share, dtype=jnp.int32)
    column_ids = jnp.arange(columns, dtype=jnp.int32)
    keep_mask = ((row_ids[:, None] < left_dims[0]) & (column_ids[None, :] < right_dims[0]))[None]

    def cross(step):
        return [
            (n * SPINS + p, (n + step) * SPINS + (p ^ 1))
            for n in range(lines)
            for p in range(SPINS)
            if 0 <= n + step < lines
        ]

    relay = [
        (n * SPINS + p, n * SPINS + p + (-2 if p % 2 else 2))
        for n in range(lines)
        for p in range(SPINS)
        if 0 <= p + (-2 if p % 2 else 2) < SPINS
    ]
    relay_here = jnp.where(odd, spin + 2 < SPINS, spin >= 2)
    from_below = (jnp.where(odd, 1, 3), jnp.where(odd, 3, 1), line > 0)
    from_above = (jnp.where(odd, 4, 2), jnp.where(odd, 2, 4), line + 1 < lines)
    if lines == 2:
        ways_across = [(cross(1) + cross(-1), tuple(jnp.where(line == 1, b, a) for b, a in zip(from_below, from_above)))]
    else:
        ways_across = [(cross(1), from_below), (cross(-1), from_above)] if lines > 1 else []
    classes = []
    for _, (near_class, far_class, valid) in ways_across:
        classes += [jnp.where(valid, near_class, -1), jnp.where(valid & relay_here, far_class, -1)]
    live_classes = [
        functools.reduce(jnp.logical_or, [found == c for found in classes], jnp.bool_(c == 0)) for c in range(CLASSES)
    ]
    meta = jnp.stack([place, left_dims[0], right_dims[0], *live_classes, *classes]).astype(jnp.int32)
    terms = functools.partial(call_terms, term_shift, meta)

    eighth = vectors // 8
    widths = [part * eighth for part in RUNS] if vectors % 8 == 0 else [vectors]
    starts = [sum(widths[:i]) for i in range(len(widths))]
    last = len(widths) - 1
    groups = [[0], list(range(1, last + 1))] if last else [[0]]
    live = call_mask(meta, wavefunction, starts, widths)
    extras = ()
    if ways == 2 and SPARE:
        packed = call_pack(term_shift, meta, left_env, right_env, ways, live[-1])
        extras = [permute(part, "mpo", [(0, 1), (1, 0)]) for part in packed]
    landed, relayed, near, far, held = {}, {}, {}, {}, {}

    def send(index, tick=None):
        block = live[index]
        if tick is not None:
            block, tick = after(block, tick)
            held.setdefault((index, 0), []).append(tick)
        landed[index] = [permute(block, "sec", pairs) for pairs, _ in ways_across]

    def receive(index, tick):
        near[index], relayed[index] = [], []
        for block in landed[index]:
            block, passed = after(block, tick)
            held.setdefault((index, 0), []).append(passed)
            near[index].append(around(block))
            relayed[index].append(permute(block, "sec", relay))

    def share_far(index, tick=None):
        far[index] = []
        for part in relayed[index]:
            if tick is not None:
                part, passed = after(part, tick)
                held.setdefault((index, 1), []).append(passed)
            far[index].append(around(part))

    def add(members, total, positions, ticks):
        ticks = list(ticks)
        for way in range(len(ways_across)):
            kinds = [OWN + 2 * way + position for position in positions]
            sources = [[(far if position else near)[index][way] for index in members] for position in positions]
            waits = ticks + [t for position in positions for index in members for t in held.get((index, position), [])]
            finish = 1 in positions and way == len(ways_across) - 1
            *total, tick = terms(kinds, sources, left_env, right_env, extras, waits, total, finish=finish)
            ticks = [tick]
            if not finish:
                total = total[0]
        return total, ticks[0]

    send(0)
    split = [sum(widths[index] for index in group) for group in groups]
    *totals, tick = terms([None], [[around(wavefunction[0])]], left_env, right_env, extras, mask=True, split=split)
    if last:
        send(1, tick)
    if ways_across:
        receive(0, tick)
        total, tick = add([0], totals[0], (0,), [tick])
        share_far(0, tick)
        if last:
            receive(1, tick)
        if last > 1:
            send(2, tick)
        totals[0], tick = add([0], total, (1,), [tick])
        if last:
            if last > 1:
                receive(2, tick)
            share_far(1, tick)
            total, tick = add(groups[1], totals[1], (0,), [tick])
            if last > 1:
                share_far(2, tick)
            totals[1], tick = add(groups[1], total, (1,), [tick])

    product = jnp.zeros_like(wavefunction[0])
    for number, group in enumerate(groups):
        sums, *gifts = totals[number] if ways_across else (totals[number][:, :share],)
        for turn, given in enumerate(gifts, 1):
            sums += permute(given, "mpo", [(i, (i + turn) % ways) for i in range(ways)]).astype(jnp.float32)
        block = jnp.where(keep_mask, sums, jnp.zeros_like(sums)).astype(jnp.bfloat16)
        product = lax.dynamic_update_slice(product, block, (starts[group[0]], 0, 0))
    return product[None]


def solution(mesh):
    in_specs = (
        P("sec", None, "mpo", None),
        P("sec", "mpo", None, None),
        P("sec", "mpo", None, None),
        P("sec"),
        P("sec"),
        P("mpo"),
    )
    out_specs = P("sec", None, "mpo", None)
    return jax.shard_map(
        per_device, mesh=mesh, in_specs=in_specs, out_specs=out_specs, check_vma=False
    )
```
